32 devices in a mesh: grp: 2 (over y), row: 8 (over z, core), chan: 2 (over x).
Axes of the slice: x: 2, y: 2, z: 4, core: 2. Of those that a mesh axis runs over, the one named last changes fastest.
Arguments:
- pair: bfloat16 [1024, 512, 128], P(('grp', 'row'), 'chan'), parts along dimension 0, may hold values from -6 to 6
- pair_mask: int32 [1024, 512], P(('grp', 'row'), 'chan'), parts along dimension 0, may hold values 0 or 1
- chain_ids: int32 [1024], P('grp'), parts along dimension 0, may hold values from 0 to 5, never falling along the last dimension, each value on 1 to 128 neighbouring positions
- chain_embed: float32 [2, 128], replicated, may hold values from -4 to 4
- proj_weights: bfloat16 [2, 128, 512], replicated, may hold values from -0.5 to 0.5
- gate_weights: bfloat16 [2, 128, 128], replicated, may hold values from -0.5 to 0.5
- out_weights: bfloat16 [2, 128, 128], replicated, may hold values from -0.5 to 0.5
Outputs:
- updated: bfloat16 [1024, 512, 128], P(('grp', 'row'), 'chan'), parts along dimension 0
The draws below stay inside these ranges and needn't reach their ends.
There are 2 independent parts, one for each index of `grp`. The reference program is written for one: setup_inputs(seed, part) draws one part's arguments, and reference() takes and returns one part's arrays. A program takes and returns all parts, laid end to end along the dimension named above; an argument that names none is the same for every part. Nothing has to cross between parts.
All inputs are finite; a program needn't handle non-finite values. No bound on the sum of `pair_mask` on one device may be relied on, other than what follows from the above.
Results may differ from the reference program's by a relative error of at most 0.0039.
Values may be sent and summed in bfloat16 or wider, within the bound.
No kernel may reach another device: no remote copies, remote signals or barrier semaphores. Data moves between devices by JAX's collectives and lax.ppermute only.
A program may use at most 128 MiB of HBM per device.

```python
import math
import jax
import jax.numpy as jnp
import numpy as np
from jax import lax

C = 128
CH = 128
ROWS_DEV = 64
N = 512


def set_ends(result, rng, low, largest):
    spot = [jax.random.randint(jax.random.fold_in(rng, axis), (), 0, length) for axis, length in enumerate(result.shape)]
    longest = result.shape.index(max(result.shape))
    next_to = spot[:longest] + [(spot[longest] + 1) % result.shape[longest]] + spot[longest + 1:]
    return result.at[tuple(spot)].set(low).at[tuple(next_to)].set(largest)


def steps_of(stream_key, dims, cuts, smallest, top_value):
    factor_of, own = 1.0, jax.random.fold_in(stream_key, 6)
    for axis_at, parts in cuts:
        heights = jnp.exp(jax.random.uniform(jax.random.fold_in(own, axis_at), (parts,), jnp.float32, smallest / len(cuts), top_value / len(cuts)))
        factor_of = factor_of * jnp.repeat(heights, dims[axis_at] // parts).reshape([-1 if axis == axis_at else 1 for axis in range(len(dims))])
    return factor_of


def length_profile(number_of, total, bound, lean):
    portions = [(1 << 20) // math.isqrt(rank ** lean) + 1 for rank in range(2, number_of + 1)]
    surplus, counts = total - bound - (number_of - 1), [1] * (number_of - 1)
    while surplus > 0:
        candidates = [i for i in range(number_of - 1) if counts[i] < bound]
        pool, left = sum([portions[i] for i in candidates]), surplus
        for i in candidates:
            more = min(bound - counts[i], max(1, left * portions[i] // pool), surplus)
            counts[i] = counts[i] + more
            surplus = surplus - more
    return np.array([bound] + counts)


def ragged(own_key, amount, total, limit, skew):
    if amount == 2:
        one = jax.random.randint(own_key, (), max(1, total - limit), min(limit, total - 1) + 1)
        return jnp.stack([one, total - one])
    tallies = jnp.asarray(length_profile(amount, total, limit, skew), jnp.int32)
    couples = (amount - 1) // 2
    donor, receiver = tallies[1:1 + 2 * couples:2], tallies[2:2 + 2 * couples:2]
    room = jnp.minimum(donor - 1, limit - receiver)
    passed = jax.random.randint(jax.random.fold_in(own_key, 1), (couples,), 0, 1 << 20) % (room + 1)
    tallies = tallies.at[1:1 + 2 * couples:2].set(donor - passed).at[2:2 + 2 * couples:2].set(receiver + passed)
    return tallies[jax.random.permutation(jax.random.fold_in(own_key, 2), amount)]


def normal_values(own_key, dims, scale, reach, shards=(), held_as=jnp.bfloat16):
    array = scale * jax.random.normal(own_key, dims, jnp.float32)
    if shards:
        array = array * steps_of(own_key, dims, shards, -0.22, 0.18)
    return jnp.clip(array, -reach, reach).astype(held_as)


def setup_inputs(seed: int = 0, part: int = 0) -> dict:
    arg_keys = jax.random.split(jax.random.key(seed), 8)
    part_keys = jax.random.split(jax.random.fold_in(arg_keys[7], part), 8)
    return {
        "pair": normal_values(part_keys[0], (N, N, C), 1.0, 6.0, ((0, 8), (1, 2))),
        "pair_mask": set_ends((jax.random.randint(part_keys[1], (N, N), 0, 10) < 9).astype(jnp.int32), jax.random.fold_in(part_keys[1], 1), 0, 1),
        "chain_ids": jnp.searchsorted(jnp.cumsum(ragged(part_keys[2], 6, N, N // 4, 1)), jnp.arange(N), side="right").astype(jnp.int32),
        "chain_embed": normal_values(arg_keys[3], (2, C), 1.0, 4.0, (), jnp.float32),
        "proj_weights": normal_values(arg_keys[4], (2, C, 4 * CH), C ** -0.5, 0.5),
        "gate_weights": normal_values(arg_keys[5], (2, C, C), C ** -0.5, 0.5),
        "out_weights": normal_values(arg_keys[6], (2, CH, C), CH ** -0.5, 0.5),
    }


def layer_norm(values, axis):
    mean = lax.optimization_barrier(jnp.mean(values, axis=axis, keepdims=True))
    centred = values - mean
    variance = lax.optimization_barrier(jnp.mean(centred * centred, axis=axis, keepdims=True))
    return centred * lax.rsqrt(variance + 1e-05)

def reference(pair, pair_mask, chain_ids, chain_embed, proj_weights, gate_weights, out_weights):
    same_chain = chain_ids[:, None] == chain_ids[None, :]
    state = pair.astype(jnp.float32) + jnp.where(same_chain[..., None], chain_embed[1], chain_embed[0])
    mask_values = pair_mask.astype(jnp.float32)
    blocks = N // ROWS_DEV
    for update in range(2):

        def project(pieces):
            state_rows, mask_rows = pieces
            normed = layer_norm(state_rows, -1).astype(jnp.bfloat16)
            flat = normed.reshape(-1, C)
            proj = jnp.dot(flat, proj_weights[update], preferred_element_type=jnp.float32).reshape(ROWS_DEV, N, 4 * CH)
            left = jax.nn.sigmoid(proj[..., :CH]) * proj[..., CH:2 * CH] * mask_rows[..., None]
            right = jax.nn.sigmoid(proj[..., 2 * CH:3 * CH]) * proj[..., 3 * CH:] * mask_rows[..., None]
            gate = jax.nn.sigmoid(jnp.dot(flat, gate_weights[update], preferred_element_type=jnp.float32)).reshape(ROWS_DEV, N, C)
            return (jnp.transpose(left, (2, 0, 1)).astype(jnp.bfloat16), jnp.transpose(right, (2, 0, 1)).astype(jnp.bfloat16), gate)
        left, right, gates = lax.map(project, (state.reshape(blocks, ROWS_DEV, N, C), mask_values.reshape(blocks, ROWS_DEV, N)))
        left = jnp.transpose(left, (1, 0, 2, 3)).reshape(CH, N, N)
        right = jnp.transpose(right, (1, 0, 2, 3)).reshape(CH, N, N)

        def product(pieces):
            left_one, right_one = pieces
            if update == 0:
                return jnp.dot(left_one, right_one.T, preferred_element_type=jnp.float32).astype(jnp.bfloat16)
            return jnp.dot(left_one.T, right_one, preferred_element_type=jnp.float32).astype(jnp.bfloat16)
        mixed = lax.map(product, (left, right))
        mixed_blocks = jnp.transpose(mixed.reshape(CH, blocks, ROWS_DEV, N), (1, 0, 2, 3))

        def finish(pieces):
            mixed_rows, state_rows, gate_rows = pieces
            mixnorm = layer_norm(jnp.transpose(mixed_rows, (1, 2, 0)).astype(jnp.float32), -1).astype(jnp.bfloat16)
            change = jnp.dot(mixnorm.reshape(-1, CH), out_weights[update], preferred_element_type=jnp.float32).reshape(ROWS_DEV, N, C)
            return state_rows + gate_rows * change
        state = lax.map(finish, (mixed_blocks, state.reshape(blocks, ROWS_DEV, N, C), gates)).reshape(N, N, C)
    return state.astype(jnp.bfloat16)
```

```python
import functools

import jax
import jax.numpy as jnp
from jax import lax
from jax.experimental import pallas as pl
from jax.experimental.pallas import tpu as pltpu
from jax.sharding import PartitionSpec as P

EPS = 1e-05
LANES = 128
VMEM = 56 * 1024 * 1024


def sigmoid(x):
    return 0.5 * jnp.tanh(0.5 * x) + 0.5


def norm_channels(values):
    scale = 1.0 / values.shape[0]
    mean = jnp.sum(values, axis=0, keepdims=True) * scale
    centred = values - mean
    variance = jnp.sum(centred * centred, axis=0, keepdims=True) * scale
    return centred * lax.rsqrt(variance + EPS)


def dot(a, b):
    return jnp.dot(a, b, preferred_element_type=jnp.float32)


def first_state(pair_ref, same_row, embed_ref, eye_ref, i):
    turned = lax.dot_general(
        eye_ref[...], pair_ref[i], (((1,), (1,)), ((), ())), preferred_element_type=jnp.float32
    )
    return turned + jnp.where(same_row, embed_ref[:, 1:2], embed_ref[:, 0:1])


def put_row(scratch, i, rows, values):
    for part in range(values.shape[1] // LANES):
        scratch[part, pl.ds(i, values.shape[0], stride=rows), :] = values[
            :, part * LANES : (part + 1) * LANES
        ]


def get_row(scratch, i, rows, channels):
    return jnp.concatenate(
        [scratch[part, pl.ds(i, channels, stride=rows), :] for part in range(scratch.shape[0])],
        axis=1,
    )


def project_row(normed, mask_row, weight_ref, left_scr, right_scr, i, rows):
    hidden = weight_ref.shape[0] // 4
    proj = dot(weight_ref[...], normed)
    put_row(left_scr, i, rows, sigmoid(proj[:hidden]) * proj[hidden : 2 * hidden] * mask_row)
    put_row(
        right_scr, i, rows, sigmoid(proj[2 * hidden : 3 * hidden]) * proj[3 * hidden :] * mask_row
    )


def write_sides(left_scr, right_scr, out_ref):
    targets, _, share, rows, cols = out_ref.shape
    for side, scratch in enumerate((left_scr, right_scr)):
        for part in range(cols // LANES):
            out_ref[:, side, :, :, part * LANES : (part + 1) * LANES] = (
                scratch[part].astype(jnp.bfloat16).reshape(targets, share, rows, LANES)
            )


def read_mixed(mixed_ref, scratch):
    for part in range(scratch.shape[0]):
        scratch[part] = (
            mixed_ref[:, :, part * LANES : (part + 1) * LANES]
            .astype(jnp.float32)
            .reshape(scratch.shape[1:])
        )


def start_kernel(
    row_chain, pair_ref, mask_ref, col_chain, embed_ref, eye_ref, proj_ref, out_ref, left_scr, right_scr
):
    rows = pair_ref.shape[0]
    step = pl.program_id(0)

    @pl.loop(0, rows)
    def _(i):
        same = col_chain[...] == row_chain[step * rows + i]
        state = first_state(pair_ref, same, embed_ref, eye_ref, i)
        normed = norm_channels(state).astype(jnp.bfloat16)
        mask_row = mask_ref[pl.ds(i, 1), :].astype(jnp.float32)
        project_row(normed, mask_row, proj_ref, left_scr, right_scr, i, rows)

    write_sides(left_scr, right_scr, out_ref)


def middle_kernel(
    row_chain, mixed_ref, pair_ref, mask_ref, col_chain, embed_ref, eye_ref, gate_ref, back_ref, proj_ref,
    state_ref, out_ref, mixed_scr, left_scr, right_scr,
):
    rows = pair_ref.shape[0]
    channels = mixed_ref.shape[0]
    step = pl.program_id(0)
    read_mixed(mixed_ref, mixed_scr)

    @pl.loop(0, rows)
    def _(i):
        same = col_chain[...] == row_chain[step * rows + i]
        state = first_state(pair_ref, same, embed_ref, eye_ref, i)
        normed = norm_channels(state).astype(jnp.bfloat16)
        gate = sigmoid(dot(gate_ref[...], normed))
        mixnorm = norm_channels(get_row(mixed_scr, i, rows, channels)).astype(jnp.bfloat16)
        state = state + gate * dot(back_ref[...], mixnorm)
        state_ref[i] = state
        normed = norm_channels(state).astype(jnp.bfloat16)
        mask_row = mask_ref[pl.ds(i, 1), :].astype(jnp.float32)
        project_row(normed, mask_row, proj_ref, left_scr, right_scr, i, rows)

    write_sides(left_scr, right_scr, out_ref)


def end_kernel(mixed_ref, state_ref, gate_ref, back_ref, out_ref, mixed_scr):
    rows = state_ref.shape[0]
    channels = mixed_ref.shape[0]
    read_mixed(mixed_ref, mixed_scr)

    @pl.loop(0, rows)
    def _(i):
        state = state_ref[i]
        normed = norm_channels(state).astype(jnp.bfloat16)
        gate = sigmoid(dot(gate_ref[...], normed))
        mixnorm = norm_channels(get_row(mixed_scr, i, rows, channels)).astype(jnp.bfloat16)
        state = state + gate * dot(back_ref[...], mixnorm)
        out_ref[i] = state.T.astype(jnp.bfloat16)


def whole(array):
    return pl.BlockSpec(array.shape, lambda *_: (0,) * array.ndim)


def params():
    return pltpu.CompilerParams(vmem_limit_bytes=VMEM)


def scratches(count, channels, rows, cols):
    return [pltpu.VMEM((cols // LANES, channels * rows, LANES), jnp.float32)] * count


SMEM_SPEC = pl.BlockSpec(memory_space=pltpu.SMEM)


def start_call(row_chain, pair, mask, col_chain, embed, eye, proj, targets, block):
    rows, cols, width = pair.shape
    hidden = proj.shape[0] // 4
    share = hidden // targets
    return pl.pallas_call(
        start_kernel,
        grid=(rows // block,),
        in_specs=[
            SMEM_SPEC,
            pl.BlockSpec((block, cols, width), lambda s: (s, 0, 0)),
            pl.BlockSpec((block, cols), lambda s: (s, 0)),
            whole(col_chain),
            whole(embed),
            whole(eye),
            whole(proj),
        ],
        out_specs=pl.BlockSpec((targets, 2, share, block, cols), lambda s: (0, 0, 0, s, 0)),
        out_shape=jax.ShapeDtypeStruct((targets, 2, share, rows, cols), jnp.bfloat16),
        scratch_shapes=scratches(2, hidden, block, cols),
        compiler_params=params(),
    )(row_chain, pair, mask, col_chain, embed, eye, proj)


def middle_call(row_chain, mixed, pair, mask, col_chain, embed, eye, gate, back, proj, targets, block):
    rows, cols, width = pair.shape
    hidden = proj.shape[0] // 4
    share = hidden // targets
    return pl.pallas_call(
        middle_kernel,
        grid=(rows // block,),
        in_specs=[
            SMEM_SPEC,
            pl.BlockSpec((hidden, block, cols), lambda s: (0, s, 0)),
            pl.BlockSpec((block, cols, width), lambda s: (s, 0, 0)),
            pl.BlockSpec((block, cols), lambda s: (s, 0)),
            whole(col_chain),
            whole(embed),
            whole(eye),
            whole(gate),
            whole(back),
            whole(proj),
        ],
        out_specs=[
            pl.BlockSpec((block, width, cols), lambda s: (s, 0, 0)),
            pl.BlockSpec((targets, 2, share, block, cols), lambda s: (0, 0, 0, s, 0)),
        ],
        out_shape=[
            jax.ShapeDtypeStruct((rows, width, cols), jnp.float32),
            jax.ShapeDtypeStruct((targets, 2, share, rows, cols), jnp.bfloat16),
        ],
        scratch_shapes=scratches(3, hidden, block, cols),
        compiler_params=params(),
    )(row_chain, mixed, pair, mask, col_chain, embed, eye, gate, back, proj)


def end_call(mixed, state, gate, back, block):
    rows, width, cols = state.shape
    hidden = mixed.shape[0]
    return pl.pallas_call(
        end_kernel,
        grid=(rows // block,),
        in_specs=[
            pl.BlockSpec((hidden, block, cols), lambda s: (0, s, 0)),
            pl.BlockSpec((block, width, cols), lambda s: (s, 0, 0)),
            whole(gate),
            whole(back),
        ],
        out_specs=pl.BlockSpec((block, cols, width), lambda s: (s, 0, 0)),
        out_shape=jax.ShapeDtypeStruct((rows, cols, width), jnp.bfloat16),
        scratch_shapes=scratches(1, hidden, block, cols),
        compiler_params=params(),
    )(mixed, state, gate, back)


def product_kernel(update, sides_ref, out_ref):
    row_parts, col_parts, _, _, rows, cols = sides_ref.shape
    size = row_parts * rows

    def side(which, part):
        return sides_ref[:, part, which, 0].reshape(size, cols)

    if update == 0:
        total = None
        for part in range(col_parts):
            term = lax.dot_general(
                side(0, part), side(1, part), (((1,), (1,)), ((), ())),
                preferred_element_type=jnp.float32,
            )
            total = term if total is None else total + term
        mixed = total.astype(jnp.bfloat16)
        for part in range(col_parts):
            out_ref[:, part, 0] = mixed[:, part * cols : (part + 1) * cols].reshape(
                row_parts, rows, cols
            )
    else:
        left = jnp.concatenate([side(0, part) for part in range(col_parts)], axis=1)
        for part in range(col_parts):
            mixed = lax.dot_general(
                left, side(1, part), (((0,), (0,)), ((), ())), preferred_element_type=jnp.float32
            ).astype(jnp.bfloat16)
            out_ref[:, part, 0] = mixed.reshape(row_parts, rows, cols)


def product_call(sides, update, row_parts, col_parts):
    targets, _, share, rows, cols = sides.shape
    sides = sides.reshape(row_parts, col_parts, 2, share, rows, cols)
    out = pl.pallas_call(
        functools.partial(product_kernel, update),
        grid=(share,),
        in_specs=[
            pl.BlockSpec((row_parts, col_parts, 2, 1, rows, cols), lambda s: (0, 0, 0, s, 0, 0))
        ],
        out_specs=pl.BlockSpec((row_parts, col_parts, 1, rows, cols), lambda s: (0, 0, s, 0, 0)),
        out_shape=jax.ShapeDtypeStruct((row_parts, col_parts, share, rows, cols), jnp.bfloat16),
        compiler_params=params(),
    )(sides)
    return out.reshape(targets, share, rows, cols)


def exchange(array):
    return lax.all_to_all(array, ("row", "chan"), split_axis=0, concat_axis=0, tiled=True)


def local(mesh, pair, pair_mask, chain_ids, chain_embed, proj_weights, gate_weights, out_weights):
    rows, cols, width = pair.shape
    row_parts, col_parts = mesh.shape["row"], mesh.shape["chan"]
    targets = row_parts * col_parts
    hidden = out_weights.shape[1]
    block = 16
    row_chain = lax.dynamic_slice_in_dim(chain_ids, lax.axis_index("row") * rows, rows)
    col_chain = lax.dynamic_slice_in_dim(chain_ids, lax.axis_index("chan") * cols, cols)[None, :]
    embed = chain_embed.T
    eye = jnp.eye(width, dtype=jnp.bfloat16)
    proj, gate, back = (
        jnp.swapaxes(weight, 1, 2) for weight in (proj_weights, gate_weights, out_weights)
    )

    sides = start_call(row_chain, pair, pair_mask, col_chain, embed, eye, proj[0], targets, block)
    mixed = exchange(product_call(exchange(sides), 0, row_parts, col_parts))
    state, sides = middle_call(
        row_chain, mixed.reshape(hidden, rows, cols), pair, pair_mask, col_chain, embed, eye,
        gate[0], back[0], proj[1], targets, block,
    )
    mixed = exchange(product_call(exchange(sides), 1, row_parts, col_parts))
    return end_call(mixed.reshape(hidden, rows, cols), state, gate[1], back[1], block)


def solution(mesh):
    placed = (
        P(("grp", "row"), "chan", None),
        P(("grp", "row"), "chan"),
        P("grp"),
        P(),
        P(),
        P(),
        P(),
    )
    return jax.shard_map(
        functools.partial(local, mesh),
        mesh=mesh,
        in_specs=placed,
        out_specs=P(("grp", "row"), "chan", None),
        check_vma=False,
    )
```

```python
import functools

import jax
import jax.numpy as jnp
from jax import lax
from jax.experimental import pallas as pl
from jax.experimental.pallas import tpu as pltpu
from jax.sharding import PartitionSpec as P

EPS = 1e-05
LANES = 128
VMEM = 56 * 1024 * 1024


def sigmoid(x):
    return 0.5 * jnp.tanh(0.5 * x) + 0.5


def norm_channels(values):
    scale = 1.0 / values.shape[0]
    mean = jnp.sum(values, axis=0, keepdims=True) * scale
    centred = values - mean
    variance = jnp.sum(centred * centred, axis=0, keepdims=True) * scale
    return centred * lax.rsqrt(variance + EPS)


def dot(a, b):
    return jnp.dot(a, b, preferred_element_type=jnp.float32)


def first_state(pair_ref, same_row, embed_ref, i):
    turned = pair_ref[i].astype(jnp.float32).T
    return turned + jnp.where(same_row, embed_ref[:, 1:2], embed_ref[:, 0:1])


def put_row(scratch, i, rows, values):
    for part in range(values.shape[1] // LANES):
        scratch[part, pl.ds(i, values.shape[0], stride=rows), :] = values[
            :, part * LANES : (part + 1) * LANES
        ]


def get_row(scratch, i, rows, channels):
    return jnp.concatenate(
        [scratch[part, pl.ds(i, channels, stride=rows), :] for part in range(scratch.shape[0])],
        axis=1,
    )


def project_row(normed, mask_row, weight_ref, left_scr, right_scr, i, rows):
    hidden = weight_ref.shape[0] // 4
    proj = dot(weight_ref[...], normed)
    put_row(left_scr, i, rows, sigmoid(proj[:hidden]) * proj[hidden : 2 * hidden] * mask_row)
    put_row(
        right_scr, i, rows, sigmoid(proj[2 * hidden : 3 * hidden]) * proj[3 * hidden :] * mask_row
    )


def write_sides(left_scr, right_scr, out_ref):
    targets, _, share, rows, cols = out_ref.shape
    for side, scratch in enumerate((left_scr, right_scr)):
        for part in range(cols // LANES):
            out_ref[:, side, :, :, part * LANES : (part + 1) * LANES] = (
                scratch[part].astype(jnp.bfloat16).reshape(targets, share, rows, LANES)
            )


def read_mixed(mixed_ref, scratch):
    for part in range(scratch.shape[0]):
        scratch[part] = (
            mixed_ref[:, :, part * LANES : (part + 1) * LANES]
            .astype(jnp.float32)
            .reshape(scratch.shape[1:])
        )


def start_kernel(
    row_chain, pair_ref, mask_ref, col_chain, embed_ref, proj_ref, out_ref, left_scr, right_scr
):
    rows = pair_ref.shape[0]
    step = pl.program_id(0)

    @pl.loop(0, rows, unroll=4)
    def _(i):
        same = col_chain[...] == row_chain[step * rows + i]
        state = first_state(pair_ref, same, embed_ref, i)
        normed = norm_channels(state).astype(jnp.bfloat16)
        mask_row = mask_ref[pl.ds(i, 1), :].astype(jnp.float32)
        project_row(normed, mask_row, proj_ref, left_scr, right_scr, i, rows)

    write_sides(left_scr, right_scr, out_ref)


def middle_kernel(
    row_chain, mixed_ref, pair_ref, mask_ref, col_chain, embed_ref, gate_ref, back_ref, proj_ref,
    state_ref, out_ref, mixed_scr, left_scr, right_scr,
):
    rows = pair_ref.shape[0]
    channels = mixed_ref.shape[0]
    step = pl.program_id(0)
    read_mixed(mixed_ref, mixed_scr)

    @pl.loop(0, rows, unroll=4)
    def _(i):
        same = col_chain[...] == row_chain[step * rows + i]
        state = first_state(pair_ref, same, embed_ref, i)
        normed = norm_channels(state).astype(jnp.bfloat16)
        gate = sigmoid(dot(gate_ref[...], normed))
        mixnorm = norm_channels(get_row(mixed_scr, i, rows, channels)).astype(jnp.bfloat16)
        state = state + gate * dot(back_ref[...], mixnorm)
        state_ref[i] = state
        normed = norm_channels(state).astype(jnp.bfloat16)
        mask_row = mask_ref[pl.ds(i, 1), :].astype(jnp.float32)
        project_row(normed, mask_row, proj_ref, left_scr, right_scr, i, rows)

    write_sides(left_scr, right_scr, out_ref)


def end_kernel(mixed_ref, state_ref, gate_ref, back_ref, out_ref, mixed_scr):
    rows = state_ref.shape[0]
    channels = mixed_ref.shape[0]
    read_mixed(mixed_ref, mixed_scr)

    @pl.loop(0, rows, unroll=4)
    def _(i):
        state = state_ref[i]
        normed = norm_channels(state).astype(jnp.bfloat16)
        gate = sigmoid(dot(gate_ref[...], normed))
        mixnorm = norm_channels(get_row(mixed_scr, i, rows, channels)).astype(jnp.bfloat16)
        state = state + gate * dot(back_ref[...], mixnorm)
        out_ref[i] = state.T.astype(jnp.bfloat16)


def whole(array):
    return pl.BlockSpec(array.shape, lambda *_: (0,) * array.ndim)


def params():
    return pltpu.CompilerParams(vmem_limit_bytes=VMEM)


def scratches(count, channels, rows, cols):
    return [pltpu.VMEM((cols // LANES, channels * rows, LANES), jnp.float32)] * count


SMEM_SPEC = pl.BlockSpec(memory_space=pltpu.SMEM)


def start_call(row_chain, pair, mask, col_chain, embed, proj, targets, block):
    rows, cols, width = pair.shape
    hidden = proj.shape[0] // 4
    share = hidden // targets
    return pl.pallas_call(
        start_kernel,
        grid=(rows // block,),
        in_specs=[
            SMEM_SPEC,
            pl.BlockSpec((block, cols, width), lambda s: (s, 0, 0)),
            pl.BlockSpec((block, cols), lambda s: (s, 0)),
            whole(col_chain),
            whole(embed),
            whole(proj),
        ],
        out_specs=pl.BlockSpec((targets, 2, share, block, cols), lambda s: (0, 0, 0, s, 0)),
        out_shape=jax.ShapeDtypeStruct((targets, 2, share, rows, cols), jnp.bfloat16),
        scratch_shapes=scratches(2, hidden, block, cols),
        compiler_params=params(),
    )(row_chain, pair, mask, col_chain, embed, proj)


def middle_call(row_chain, mixed, pair, mask, col_chain, embed, gate, back, proj, targets, block):
    rows, cols, width = pair.shape
    hidden = proj.shape[0] // 4
    share = hidden // targets
    return pl.pallas_call(
        middle_kernel,
        grid=(rows // block,),
        in_specs=[
            SMEM_SPEC,
            pl.BlockSpec((hidden, block, cols), lambda s: (0, s, 0)),
            pl.BlockSpec((block, cols, width), lambda s: (s, 0, 0)),
            pl.BlockSpec((block, cols), lambda s: (s, 0)),
            whole(col_chain),
            whole(embed),
            whole(gate),
            whole(back),
            whole(proj),
        ],
        out_specs=[
            pl.BlockSpec((block, width, cols), lambda s: (s, 0, 0)),
            pl.BlockSpec((targets, 2, share, block, cols), lambda s: (0, 0, 0, s, 0)),
        ],
        out_shape=[
            jax.ShapeDtypeStruct((rows, width, cols), jnp.float32),
            jax.ShapeDtypeStruct((targets, 2, share, rows, cols), jnp.bfloat16),
        ],
        scratch_shapes=scratches(3, hidden, block, cols),
        compiler_params=params(),
    )(row_chain, mixed, pair, mask, col_chain, embed, gate, back, proj)


def end_call(mixed, state, gate, back, block):
    rows, width, cols = state.shape
    hidden = mixed.shape[0]
    return pl.pallas_call(
        end_kernel,
        grid=(rows // block,),
        in_specs=[
            pl.BlockSpec((hidden, block, cols), lambda s: (0, s, 0)),
            pl.BlockSpec((block, width, cols), lambda s: (s, 0, 0)),
            whole(gate),
            whole(back),
        ],
        out_specs=pl.BlockSpec((block, cols, width), lambda s: (s, 0, 0)),
        out_shape=jax.ShapeDtypeStruct((rows, cols, width), jnp.bfloat16),
        scratch_shapes=scratches(1, hidden, block, cols),
        compiler_params=params(),
    )(mixed, state, gate, back)


def product_kernel(update, sides_ref, out_ref):
    row_parts, col_parts, _, _, rows, cols = sides_ref.shape
    size = row_parts * rows

    def side(which, part):
        return sides_ref[:, part, which, 0].reshape(size, cols)

    if update == 0:
        total = None
        for part in range(col_parts):
            term = lax.dot_general(
                side(0, part), side(1, part), (((1,), (1,)), ((), ())),
                preferred_element_type=jnp.float32,
            )
            total = term if total is None else total + term
        mixed = total.astype(jnp.bfloat16)
        for part in range(col_parts):
            out_ref[:, part, 0] = mixed[:, part * cols : (part + 1) * cols].reshape(
                row_parts, rows, cols
            )
    else:
        left = jnp.concatenate([side(0, part) for part in range(col_parts)], axis=1)
        for part in range(col_parts):
            mixed = lax.dot_general(
                left, side(1, part), (((0,), (0,)), ((), ())), preferred_element_type=jnp.float32
            ).astype(jnp.bfloat16)
            out_ref[:, part, 0] = mixed.reshape(row_parts, rows, cols)


def product_call(sides, update, row_parts, col_parts):
    targets, _, share, rows, cols = sides.shape
    sides = sides.reshape(row_parts, col_parts, 2, share, rows, cols)
    out = pl.pallas_call(
        functools.partial(product_kernel, update),
        grid=(share,),
        in_specs=[
            pl.BlockSpec((row_parts, col_parts, 2, 1, rows, cols), lambda s: (0, 0, 0, s, 0, 0))
        ],
        out_specs=pl.BlockSpec((row_parts, col_parts, 1, rows, cols), lambda s: (0, 0, s, 0, 0)),
        out_shape=jax.ShapeDtypeStruct((row_parts, col_parts, share, rows, cols), jnp.bfloat16),
        compiler_params=params(),
    )(sides)
    return out.reshape(targets, share, rows, cols)


def exchange(array):
    return lax.all_to_all(array, ("row", "chan"), split_axis=0, concat_axis=0, tiled=True)


def local(mesh, pair, pair_mask, chain_ids, chain_embed, proj_weights, gate_weights, out_weights):
    rows, cols, width = pair.shape
    row_parts, col_parts = mesh.shape["row"], mesh.shape["chan"]
    targets = row_parts * col_parts
    hidden = out_weights.shape[1]
    block = 16
    row_chain = lax.dynamic_slice_in_dim(chain_ids, lax.axis_index("row") * rows, rows)
    col_chain = lax.dynamic_slice_in_dim(chain_ids, lax.axis_index("chan") * cols, cols)[None, :]
    embed = chain_embed.T
    proj, gate, back = (
        jnp.swapaxes(weight, 1, 2) for weight in (proj_weights, gate_weights, out_weights)
    )

    sides = start_call(row_chain, pair, pair_mask, col_chain, embed, proj[0], targets, block)
    mixed = exchange(product_call(exchange(sides), 0, row_parts, col_parts))
    state, sides = middle_call(
        row_chain, mixed.reshape(hidden, rows, cols), pair, pair_mask, col_chain, embed,
        gate[0], back[0], proj[1], targets, block,
    )
    mixed = exchange(product_call(exchange(sides), 1, row_parts, col_parts))
    return end_call(mixed.reshape(hidden, rows, cols), state, gate[1], back[1], block)


def solution(mesh):
    placed = (
        P(("grp", "row"), "chan", None),
        P(("grp", "row"), "chan"),
        P("grp"),
        P(),
        P(),
        P(),
        P(),
    )
    return jax.shard_map(
        functools.partial(local, mesh),
        mesh=mesh,
        in_specs=placed,
        out_specs=P(("grp", "row"), "chan", None),
        check_vma=False,
    )
```

```python
import functools

import jax
import jax.numpy as jnp
from jax import lax
from jax.experimental import pallas as pl
from jax.experimental.pallas import tpu as pltpu
from jax.sharding import PartitionSpec as P

EPS = 1e-05
LANES = 128
VMEM = 56 * 1024 * 1024
FIRST, MIDDLE, LAST = (4, 12), (4, 12), (12, 4)


def sigmoid(x):
    return 0.5 * jnp.tanh(0.5 * x) + 0.5


def norm_channels(values):
    scale = 1.0 / values.shape[0]
    mean = jnp.sum(values, axis=0, keepdims=True) * scale
    centred = values - mean
    variance = jnp.sum(centred * centred, axis=0, keepdims=True) * scale
    return centred * lax.rsqrt(variance + EPS)


def dot(a, b):
    return jnp.dot(a, b, preferred_element_type=jnp.float32)


def same_chain(chains, chain_row, cols, rows, i):
    start = pl.multiple_of(lax.axis_index("chan") * cols, cols)
    return chain_row[:, pl.ds(start, cols)] == chains[lax.axis_index("row") * rows + i]


def first_state(pair_ref, same_row, embed_ref, i):
    turned = pair_ref[i].astype(jnp.float32).T
    return turned + jnp.where(same_row, embed_ref[:, 1:2], embed_ref[:, 0:1])


def put_row(scratch, i, rows, values):
    for part in range(values.shape[1] // LANES):
        scratch[part, pl.ds(i, values.shape[0], stride=rows), :] = values[
            :, part * LANES : (part + 1) * LANES
        ]


def get_row(scratch, i, rows, channels):
    return jnp.concatenate(
        [scratch[part, pl.ds(i, channels, stride=rows), :] for part in range(scratch.shape[0])],
        axis=1,
    )


def project_row(normed, mask_row, weight_ref, left_scr, right_scr, i, rows):
    hidden = weight_ref.shape[0] // 4
    proj = dot(weight_ref[...], normed)
    put_row(left_scr, i, rows, sigmoid(proj[:hidden]) * proj[hidden : 2 * hidden] * mask_row)
    put_row(
        right_scr, i, rows, sigmoid(proj[2 * hidden : 3 * hidden]) * proj[3 * hidden :] * mask_row
    )


def write_sides(left_scr, right_scr, out_ref):
    targets, _, share, rows, cols = out_ref.shape
    for side, scratch in enumerate((left_scr, right_scr)):
        for part in range(cols // LANES):
            out_ref[:, side, :, :, part * LANES : (part + 1) * LANES] = (
                scratch[part].astype(jnp.bfloat16).reshape(targets, share, rows, LANES)
            )


def read_mixed(mixed_ref, scratch):
    for part in range(scratch.shape[0]):
        scratch[part] = (
            mixed_ref[:, :, part * LANES : (part + 1) * LANES]
            .astype(jnp.float32)
            .reshape(scratch.shape[1:])
        )


def start_kernel(
    first, total_rows, row_chain, pair_ref, mask_ref, col_chain, embed_ref, proj_ref, out_ref, left_scr, right_scr
):
    rows = pair_ref.shape[0]
    step = pl.program_id(0) + first

    @pl.loop(0, rows, unroll=4)
    def _(i):
        same = same_chain(row_chain, col_chain, pair_ref.shape[1], total_rows, step * rows + i)
        state = first_state(pair_ref, same, embed_ref, i)
        normed = norm_channels(state).astype(jnp.bfloat16)
        mask_row = mask_ref[pl.ds(i, 1), :].astype(jnp.float32)
        project_row(normed, mask_row, proj_ref, left_scr, right_scr, i, rows)

    write_sides(left_scr, right_scr, out_ref)


def middle_kernel(
    first, total_rows, row_chain, mixed_ref, pair_ref, mask_ref, col_chain, embed_ref, gate_ref, back_ref, proj_ref,
    state_ref, out_ref, mixed_scr, left_scr, right_scr,
):
    rows = pair_ref.shape[0]
    channels = mixed_ref.shape[0]
    step = pl.program_id(0) + first
    read_mixed(mixed_ref, mixed_scr)

    @pl.loop(0, rows, unroll=4)
    def _(i):
        same = same_chain(row_chain, col_chain, pair_ref.shape[1], total_rows, step * rows + i)
        state = first_state(pair_ref, same, embed_ref, i)
        normed = norm_channels(state).astype(jnp.bfloat16)
        gate = sigmoid(dot(gate_ref[...], normed))
        mixnorm = norm_channels(get_row(mixed_scr, i, rows, channels)).astype(jnp.bfloat16)
        state = state + gate * dot(back_ref[...], mixnorm)
        state_ref[i] = state
        normed = norm_channels(state).astype(jnp.bfloat16)
        mask_row = mask_ref[pl.ds(i, 1), :].astype(jnp.float32)
        project_row(normed, mask_row, proj_ref, left_scr, right_scr, i, rows)

    write_sides(left_scr, right_scr, out_ref)


def end_kernel(mixed_ref, state_ref, gate_ref, back_ref, out_ref, mixed_scr):
    rows = state_ref.shape[0]
    channels = mixed_ref.shape[0]
    read_mixed(mixed_ref, mixed_scr)

    @pl.loop(0, rows, unroll=4)
    def _(i):
        state = state_ref[i]
        normed = norm_channels(state).astype(jnp.bfloat16)
        gate = sigmoid(dot(gate_ref[...], normed))
        mixnorm = norm_channels(get_row(mixed_scr, i, rows, channels)).astype(jnp.bfloat16)
        state = state + gate * dot(back_ref[...], mixnorm)
        out_ref[i] = state.T.astype(jnp.bfloat16)


def middle_kernel_onto(first, total_rows, *refs):
    middle_kernel(first, total_rows, *refs[:9], *refs[10:])


def end_kernel_onto(mixed_ref, state_ref, gate_ref, back_ref, earlier_ref, out_ref, mixed_scr):
    del earlier_ref
    end_kernel(mixed_ref, state_ref, gate_ref, back_ref, out_ref, mixed_scr)


def cost(pairs, multiplies, bytes_each):
    return pl.CostEstimate(
        flops=2 * pairs * multiplies, bytes_accessed=pairs * bytes_each, transcendentals=0
    )


def whole(array):
    return pl.BlockSpec(array.shape, lambda *_: (0,) * array.ndim)


def params():
    return pltpu.CompilerParams(vmem_limit_bytes=VMEM)


def scratches(count, channels, rows, cols):
    return [pltpu.VMEM((cols // LANES, channels * rows, LANES), jnp.float32)] * count


SMEM_SPEC = pl.BlockSpec(memory_space=pltpu.SMEM)


def start_call(row_chain, pair, mask, col_chain, embed, proj, targets, block, first, count):
    _, cols, width = pair.shape
    hidden = proj.shape[0] // 4
    share = hidden // targets
    return pl.pallas_call(
        functools.partial(start_kernel, first, pair.shape[0]),
        grid=(count,),
        in_specs=[
            SMEM_SPEC,
            pl.BlockSpec((block, cols, width), lambda s: (s + first, 0, 0)),
            pl.BlockSpec((block, cols), lambda s: (s + first, 0)),
            whole(col_chain),
            whole(embed),
            whole(proj),
        ],
        out_specs=pl.BlockSpec((targets, 2, share, block, cols), lambda s: (0, 0, 0, s, 0)),
        out_shape=jax.ShapeDtypeStruct((targets, 2, share, count * block, cols), jnp.bfloat16),
        scratch_shapes=scratches(2, hidden, block, cols),
        compiler_params=params(),
        cost_estimate=cost(count * block * cols, 5 * width * width, 4 * width),
    )(row_chain, pair, mask, col_chain, embed, proj)


def middle_call(
    row_chain, mixed, pair, mask, col_chain, embed, gate, back, proj, targets, block, first, count, earlier
):
    rows, cols, width = pair.shape
    hidden = proj.shape[0] // 4
    share = hidden // targets
    operands = [row_chain, mixed, pair, mask, col_chain, embed, gate, back, proj]
    in_specs = [
        SMEM_SPEC,
        pl.BlockSpec((hidden, block, cols), lambda s: (0, s, 0)),
        pl.BlockSpec((block, cols, width), lambda s: (s + first, 0, 0)),
        pl.BlockSpec((block, cols), lambda s: (s + first, 0)),
        whole(col_chain),
        whole(embed),
        whole(gate),
        whole(back),
        whole(proj),
    ]
    kernel, aliases = middle_kernel, {}
    if earlier is not None:
        kernel, aliases = middle_kernel_onto, {9: 0}
        operands.append(earlier)
        in_specs.append(pl.BlockSpec(memory_space=pl.ANY))
    return pl.pallas_call(
        functools.partial(kernel, first, rows),
        grid=(count,),
        in_specs=in_specs,
        out_specs=[
            pl.BlockSpec((block, width, cols), lambda s: (s + first, 0, 0)),
            pl.BlockSpec((targets, 2, share, block, cols), lambda s: (0, 0, 0, s, 0)),
        ],
        out_shape=[
            jax.ShapeDtypeStruct((rows, width, cols), jnp.float32),
            jax.ShapeDtypeStruct((targets, 2, share, count * block, cols), jnp.bfloat16),
        ],
        scratch_shapes=scratches(3, hidden, block, cols),
        input_output_aliases=aliases,
        compiler_params=params(),
        cost_estimate=cost(count * block * cols, 8 * width * width, 12 * width),
    )(*operands)


def end_call(mixed, state, gate, back, block, first, count, rows, earlier):
    _, width, cols = state.shape
    hidden = mixed.shape[0]
    kernel = end_kernel
    operands = [mixed, state, gate, back]
    in_specs = [
        pl.BlockSpec((hidden, block, cols), lambda s: (0, s, 0)),
        pl.BlockSpec((block, width, cols), lambda s: (s + first, 0, 0)),
        whole(gate),
        whole(back),
    ]
    aliases = {}
    if earlier is not None:
        kernel = end_kernel_onto
        operands.append(earlier)
        in_specs.append(pl.BlockSpec(memory_space=pl.ANY))
        aliases = {4: 0}
    return pl.pallas_call(
        kernel,
        grid=(count,),
        in_specs=in_specs,
        out_specs=pl.BlockSpec((block, cols, width), lambda s: (s + first, 0, 0)),
        out_shape=jax.ShapeDtypeStruct((rows, cols, width), jnp.bfloat16),
        scratch_shapes=scratches(1, hidden, block, cols),
        input_output_aliases=aliases,
        compiler_params=params(),
        cost_estimate=cost(count * block * cols, 2 * width * width, 8 * width),
    )(*operands)


def product_kernel(update, lefts, rights, wanted, *refs):
    left_refs, right_refs, outs = refs[:lefts], refs[lefts : lefts + rights], refs[lefts + rights :]
    row_parts, col_parts = right_refs[0].shape[:2]
    cols = right_refs[0].shape[-1]

    def side(held, part):
        held = [ref[:, part, 0, 0] for ref in held]
        return held[0] if len(held) == 1 else jnp.concatenate(held, axis=1)

    if update == 0:
        right = [side(right_refs, part).reshape(-1, cols) for part in range(col_parts)]
        for (first, count), out in zip(wanted, outs, strict=True):
            total = None
            for part in range(col_parts):
                left = side(left_refs, part)[:, first : first + count].reshape(-1, cols)
                term = lax.dot_general(
                    left, right[part], (((1,), (1,)), ((), ())), preferred_element_type=jnp.float32
                )
                total = term if total is None else total + term
            mixed = total.astype(jnp.bfloat16).reshape(row_parts, count, -1)
            for part in range(col_parts):
                out[:, part, 0] = mixed[:, :, part * cols : (part + 1) * cols]
    else:
        left = jnp.concatenate(
            [side(left_refs, part).reshape(-1, cols) for part in range(col_parts)], axis=1
        )
        for part in range(col_parts):
            mixed = lax.dot_general(
                left, side(right_refs, part).reshape(-1, cols), (((0,), (0,)), ((), ())),
                preferred_element_type=jnp.float32,
            ).astype(jnp.bfloat16)
            mixed = mixed.reshape(row_parts, -1, cols)
            for (first, count), out in zip(wanted, outs, strict=True):
                out[:, part, 0] = mixed[:, first : first + count]


def product_call(sides, update, row_parts, col_parts, wanted):
    targets, _, share, _, cols = sides[0].shape
    sides = [side.reshape(row_parts, col_parts, 2, share, -1, cols) for side in sides]
    size = row_parts * sum(side.shape[4] for side in sides)
    lefts, shift = sides, 0
    if update == 0:
        lefts, start = [], 0
        first, last = wanted[0][0], wanted[-1][0] + wanted[-1][1]
        for side in sides:
            end = start + side.shape[4]
            if end <= first:
                shift = end
            elif start < last:
                lefts.append(side)
            start = end
    wanted = [(first - shift, count) for first, count in wanted]

    def spec(side, which):
        return pl.BlockSpec(
            (row_parts, col_parts, 1, 1, side.shape[4], cols), lambda s: (0, 0, which, s, 0, 0)
        )

    outs = pl.pallas_call(
        functools.partial(product_kernel, update, len(lefts), len(sides), wanted),
        grid=(share,),
        in_specs=[spec(side, 0) for side in lefts] + [spec(side, 1) for side in sides],
        out_specs=[
            pl.BlockSpec((row_parts, col_parts, 1, count, cols), lambda s: (0, 0, s, 0, 0))
            for _, count in wanted
        ],
        out_shape=[
            jax.ShapeDtypeStruct((row_parts, col_parts, share, count, cols), jnp.bfloat16)
            for _, count in wanted
        ],
        compiler_params=params(),
        cost_estimate=cost(share * size * size, size, 6),
    )(*lefts, *sides)
    return [out.reshape(targets, share, -1, cols) for out in outs]


def exchange(array):
    return lax.all_to_all(array, ("row", "chan"), split_axis=0, concat_axis=0, tiled=True)


def local(mesh, pair, pair_mask, chain_ids, chain_embed, proj_weights, gate_weights, out_weights):
    rows, cols, width = pair.shape
    row_parts, col_parts = mesh.shape["row"], mesh.shape["chan"]
    targets = row_parts * col_parts
    hidden = out_weights.shape[1]
    block = 16
    row_chain, col_chain = chain_ids, chain_ids[None, :]
    embed = chain_embed.T
    proj, gate, back = (
        jnp.swapaxes(weight, 1, 2) for weight in (proj_weights, gate_weights, out_weights)
    )

    def pieces(sixteenths):
        blocks, spans, start = rows // block, [], 0
        for part in sixteenths:
            count = blocks * part // 16
            spans.append((start, count))
            start += count
        return spans

    def rows_of(spans):
        return [(first * block, count * block) for first, count in spans]

    sides = [
        exchange(
            start_call(
                row_chain, pair, pair_mask, col_chain, embed, proj[0], targets, block, first, count
            )
        )
        for first, count in pieces(FIRST)
    ]
    mixed = []
    for span in rows_of(pieces(MIDDLE)):
        mixed += [exchange(part) for part in product_call(sides, 0, row_parts, col_parts, [span])]
    state, sides = None, []
    for (first, count), part in zip(pieces(MIDDLE), mixed, strict=True):
        state, part = middle_call(
            row_chain, part.reshape(hidden, -1, cols), pair, pair_mask, col_chain, embed,
            gate[0], back[0], proj[1], targets, block, first, count, state,
        )
        sides.append(exchange(part))
    mixed = [
        exchange(part)
        for part in product_call(sides, 1, row_parts, col_parts, rows_of(pieces(LAST)))
    ]
    updated = None
    for (first, count), part in zip(pieces(LAST), mixed, strict=True):
        updated = end_call(
            part.reshape(hidden, -1, cols), state, gate[1], back[1], block, first, count, rows, updated
        )
    return updated


def solution(mesh):
    placed = (
        P(("grp", "row"), "chan", None),
        P(("grp", "row"), "chan"),
        P("grp"),
        P(),
        P(),
        P(),
        P(),
    )
    return jax.shard_map(
        functools.partial(local, mesh),
        mesh=mesh,
        in_specs=placed,
        out_specs=P(("grp", "row"), "chan", None),
        check_vma=False,
    )
```

```python
import functools
import math

import jax
import jax.numpy as jnp
from jax import lax
from jax.experimental import pallas as pl
from jax.experimental.pallas import tpu as pltpu
from jax.sharding import PartitionSpec as P

EPS = 1e-05
LANES = 128
CHANNELS = 4
VMEM = 60 * 1024 * 1024
FIRST, MIDDLE, LAST = (4, 12), (4, 12), (12, 4)


def sigmoid(x):
    return 0.5 * jnp.tanh(0.5 * x) + 0.5


def norm_channels(values):
    scale = 1.0 / values.shape[0]
    mean = jnp.sum(values, axis=0, keepdims=True) * scale
    centred = values - mean
    variance = jnp.sum(centred * centred, axis=0, keepdims=True) * scale
    return centred * lax.rsqrt(variance + EPS)


def dot(a, b):
    return jnp.dot(a, b, preferred_element_type=jnp.float32)


def same_chain(chains, chain_row, cols, rows, i):
    start = pl.multiple_of(lax.axis_index("chan") * cols, cols)
    return chain_row[:, pl.ds(start, cols)] == chains[lax.axis_index("row") * rows + i]


def turn_embed(embed_ref, embed_scr):
    _, width, cols = embed_scr.shape
    for kind in range(2):
        rows = jnp.broadcast_to(embed_ref[kind : kind + 1, :], (cols, width))
        embed_scr[kind] = rows.T


def first_state(pair_ref, same_row, embed_scr, i):
    turned = pair_ref[i].astype(jnp.float32).T
    return turned + jnp.where(same_row, embed_scr[1], embed_scr[0])


def put_row(scratch, i, rows, values):
    for part in range(values.shape[1] // LANES):
        scratch[part, pl.ds(i, values.shape[0], stride=rows), :] = values[
            :, part * LANES : (part + 1) * LANES
        ]


def get_row(scratch, i, rows, channels):
    return jnp.concatenate(
        [scratch[part, pl.ds(i, channels, stride=rows), :] for part in range(scratch.shape[0])],
        axis=1,
    )


def project_row(normed, mask_row, weight_ref, left_scr, right_scr, i, rows):
    hidden = weight_ref.shape[0] // 4
    proj = dot(weight_ref[...], normed)
    put_row(left_scr, i, rows, sigmoid(proj[:hidden]) * proj[hidden : 2 * hidden] * mask_row)
    put_row(
        right_scr, i, rows, sigmoid(proj[2 * hidden : 3 * hidden]) * proj[3 * hidden :] * mask_row
    )


def write_sides(left_scr, right_scr, out_ref):
    targets, _, share, rows, cols = out_ref.shape
    for side, scratch in enumerate((left_scr, right_scr)):
        for part in range(cols // LANES):
            out_ref[:, side, :, :, part * LANES : (part + 1) * LANES] = (
                scratch[part].astype(jnp.bfloat16).reshape(targets, share, rows, LANES)
            )


def read_mixed(mixed_ref, scratch):
    for part in range(scratch.shape[0]):
        scratch[part] = (
            mixed_ref[:, :, part * LANES : (part + 1) * LANES]
            .astype(jnp.float32)
            .reshape(scratch.shape[1:])
        )


def start_kernel(
    first, total_rows, row_chain, pair_ref, mask_ref, col_chain, embed_ref, proj_ref, out_ref, left_scr, right_scr, embed_scr
):
    rows = pair_ref.shape[0]
    step = pl.program_id(0) + first
    turn_embed(embed_ref, embed_scr)

    @pl.loop(0, rows, unroll=4)
    def _(i):
        same = same_chain(row_chain, col_chain, pair_ref.shape[1], total_rows, step * rows + i)
        state = first_state(pair_ref, same, embed_scr, i)
        normed = norm_channels(state).astype(jnp.bfloat16)
        mask_row = mask_ref[pl.ds(i, 1), :].astype(jnp.float32)
        project_row(normed, mask_row, proj_ref, left_scr, right_scr, i, rows)

    write_sides(left_scr, right_scr, out_ref)


def middle_kernel(
    first, total_rows, row_chain, mixed_ref, pair_ref, mask_ref, col_chain, embed_ref, gate_ref, back_ref, proj_ref,
    state_ref, out_ref, mixed_scr, left_scr, right_scr, embed_scr,
):
    rows = pair_ref.shape[0]
    channels = mixed_ref.shape[0]
    step = pl.program_id(0) + first
    turn_embed(embed_ref, embed_scr)
    read_mixed(mixed_ref, mixed_scr)

    @pl.loop(0, rows, unroll=4)
    def _(i):
        same = same_chain(row_chain, col_chain, pair_ref.shape[1], total_rows, step * rows + i)
        state = first_state(pair_ref, same, embed_scr, i)
        normed = norm_channels(state).astype(jnp.bfloat16)
        gate = sigmoid(dot(gate_ref[...], normed))
        mixnorm = norm_channels(get_row(mixed_scr, i, rows, channels)).astype(jnp.bfloat16)
        state = state + gate * dot(back_ref[...], mixnorm)
        state_ref[i] = state
        normed = norm_channels(state).astype(jnp.bfloat16)
        mask_row = mask_ref[pl.ds(i, 1), :].astype(jnp.float32)
        project_row(normed, mask_row, proj_ref, left_scr, right_scr, i, rows)

    write_sides(left_scr, right_scr, out_ref)


def end_kernel(mixed_ref, state_ref, gate_ref, back_ref, out_ref, mixed_scr):
    rows = state_ref.shape[0]
    channels = mixed_ref.shape[0]
    read_mixed(mixed_ref, mixed_scr)

    @pl.loop(0, rows, unroll=4)
    def _(i):
        state = state_ref[i]
        normed = norm_channels(state).astype(jnp.bfloat16)
        gate = sigmoid(dot(gate_ref[...], normed))
        mixnorm = norm_channels(get_row(mixed_scr, i, rows, channels)).astype(jnp.bfloat16)
        state = state + gate * dot(back_ref[...], mixnorm)
        out_ref[i] = state.T.astype(jnp.bfloat16)


def middle_kernel_onto(first, total_rows, *refs):
    middle_kernel(first, total_rows, *refs[:9], *refs[10:])


def end_kernel_onto(mixed_ref, state_ref, gate_ref, back_ref, earlier_ref, out_ref, mixed_scr):
    del earlier_ref
    end_kernel(mixed_ref, state_ref, gate_ref, back_ref, out_ref, mixed_scr)


def cost(pairs, multiplies, bytes_each):
    return pl.CostEstimate(
        flops=2 * pairs * multiplies, bytes_accessed=pairs * bytes_each, transcendentals=0
    )


def whole(array):
    return pl.BlockSpec(array.shape, lambda *_: (0,) * array.ndim)


def params():
    return pltpu.CompilerParams(vmem_limit_bytes=VMEM)


def scratches(count, channels, rows, cols):
    return [pltpu.VMEM((cols // LANES, channels * rows, LANES), jnp.float32)] * count


SMEM_SPEC = pl.BlockSpec(memory_space=pltpu.SMEM)


def start_call(row_chain, pair, mask, col_chain, embed, proj, targets, block, first, count):
    _, cols, width = pair.shape
    hidden = proj.shape[0] // 4
    share = hidden // targets
    return pl.pallas_call(
        functools.partial(start_kernel, first, pair.shape[0]),
        grid=(count,),
        in_specs=[
            SMEM_SPEC,
            pl.BlockSpec((block, cols, width), lambda s: (s + first, 0, 0)),
            pl.BlockSpec((block, cols), lambda s: (s + first, 0)),
            whole(col_chain),
            whole(embed),
            whole(proj),
        ],
        out_specs=pl.BlockSpec((targets, 2, share, block, cols), lambda s: (0, 0, 0, s, 0)),
        out_shape=jax.ShapeDtypeStruct((targets, 2, share, count * block, cols), jnp.bfloat16),
        scratch_shapes=scratches(2, hidden, block, cols) + [pltpu.VMEM((2, width, cols), jnp.float32)],
        compiler_params=params(),
        cost_estimate=cost(count * block * cols, 5 * width * width, 4 * width),
    )(row_chain, pair, mask, col_chain, embed, proj)


def middle_call(
    row_chain, mixed, pair, mask, col_chain, embed, gate, back, proj, targets, block, first, count, earlier
):
    rows, cols, width = pair.shape
    hidden = proj.shape[0] // 4
    share = hidden // targets
    operands = [row_chain, mixed, pair, mask, col_chain, embed, gate, back, proj]
    in_specs = [
        SMEM_SPEC,
        pl.BlockSpec((hidden, block, cols), lambda s: (0, s, 0)),
        pl.BlockSpec((block, cols, width), lambda s: (s + first, 0, 0)),
        pl.BlockSpec((block, cols), lambda s: (s + first, 0)),
        whole(col_chain),
        whole(embed),
        whole(gate),
        whole(back),
        whole(proj),
    ]
    kernel, aliases = middle_kernel, {}
    if earlier is not None:
        kernel, aliases = middle_kernel_onto, {9: 0}
        operands.append(earlier)
        in_specs.append(pl.BlockSpec(memory_space=pl.ANY))
    return pl.pallas_call(
        functools.partial(kernel, first, rows),
        grid=(count,),
        in_specs=in_specs,
        out_specs=[
            pl.BlockSpec((block, width, cols), lambda s: (s + first, 0, 0)),
            pl.BlockSpec((targets, 2, share, block, cols), lambda s: (0, 0, 0, s, 0)),
        ],
        out_shape=[
            jax.ShapeDtypeStruct((rows, width, cols), jnp.float32),
            jax.ShapeDtypeStruct((targets, 2, share, count * block, cols), jnp.bfloat16),
        ],
        scratch_shapes=scratches(3, hidden, block, cols) + [pltpu.VMEM((2, width, cols), jnp.float32)],
        input_output_aliases=aliases,
        compiler_params=params(),
        cost_estimate=cost(count * block * cols, 8 * width * width, 12 * width),
    )(*operands)


def end_call(mixed, state, gate, back, block, first, count, rows, earlier):
    _, width, cols = state.shape
    hidden = mixed.shape[0]
    kernel = end_kernel
    operands = [mixed, state, gate, back]
    in_specs = [
        pl.BlockSpec((hidden, block, cols), lambda s: (0, s, 0)),
        pl.BlockSpec((block, width, cols), lambda s: (s + first, 0, 0)),
        whole(gate),
        whole(back),
    ]
    aliases = {}
    if earlier is not None:
        kernel = end_kernel_onto
        operands.append(earlier)
        in_specs.append(pl.BlockSpec(memory_space=pl.ANY))
        aliases = {4: 0}
    return pl.pallas_call(
        kernel,
        grid=(count,),
        in_specs=in_specs,
        out_specs=pl.BlockSpec((block, cols, width), lambda s: (s + first, 0, 0)),
        out_shape=jax.ShapeDtypeStruct((rows, cols, width), jnp.bfloat16),
        scratch_shapes=scratches(1, hidden, block, cols),
        input_output_aliases=aliases,
        compiler_params=params(),
        cost_estimate=cost(count * block * cols, 2 * width * width, 8 * width),
    )(*operands)


def product_kernel(update, lefts, rights, wanted, *refs):
    for channel in range(refs[0].shape[3]):
        product_channel(channel, update, lefts, rights, wanted, *refs)


def product_channel(channel, update, lefts, rights, wanted, *refs):
    left_refs, right_refs, outs = refs[:lefts], refs[lefts : lefts + rights], refs[lefts + rights :]
    row_parts, col_parts = right_refs[0].shape[:2]
    cols = right_refs[0].shape[-1]

    def side(held, part):
        held = [ref[:, part, 0, channel] for ref in held]
        return held[0] if len(held) == 1 else jnp.concatenate(held, axis=1)

    if update == 0:
        right = [side(right_refs, part).reshape(-1, cols) for part in range(col_parts)]
        for (first, count), out in zip(wanted, outs, strict=True):
            total = None
            for part in range(col_parts):
                left = side(left_refs, part)[:, first : first + count].reshape(-1, cols)
                term = lax.dot_general(
                    left, right[part], (((1,), (1,)), ((), ())), preferred_element_type=jnp.float32
                )
                total = term if total is None else total + term
            mixed = total.astype(jnp.bfloat16).reshape(row_parts, count, -1)
            for part in range(col_parts):
                out[:, part, channel] = mixed[:, :, part * cols : (part + 1) * cols]
    else:
        left = jnp.concatenate(
            [side(left_refs, part).reshape(-1, cols) for part in range(col_parts)], axis=1
        )
        for part in range(col_parts):
            mixed = lax.dot_general(
                left, side(right_refs, part).reshape(-1, cols), (((0,), (0,)), ((), ())),
                preferred_element_type=jnp.float32,
            ).astype(jnp.bfloat16)
            mixed = mixed.reshape(row_parts, -1, cols)
            for (first, count), out in zip(wanted, outs, strict=True):
                out[:, part, channel] = mixed[:, first : first + count]


def product_call(sides, update, row_parts, col_parts, wanted):
    targets, _, share, _, cols = sides[0].shape
    sides = [side.reshape(row_parts, col_parts, 2, share, -1, cols) for side in sides]
    size = row_parts * sum(side.shape[4] for side in sides)
    lefts, shift = sides, 0
    if update == 0:
        lefts, start = [], 0
        first, last = wanted[0][0], wanted[-1][0] + wanted[-1][1]
        for side in sides:
            end = start + side.shape[4]
            if end <= first:
                shift = end
            elif start < last:
                lefts.append(side)
            start = end
    wanted = [(first - shift, count) for first, count in wanted]
    step = math.gcd(share, CHANNELS)

    def spec(side, which):
        return pl.BlockSpec(
            (row_parts, col_parts, 1, step, side.shape[4], cols), lambda s: (0, 0, which, s, 0, 0)
        )

    outs = pl.pallas_call(
        functools.partial(product_kernel, update, len(lefts), len(sides), wanted),
        grid=(share // step,),
        in_specs=[spec(side, 0) for side in lefts] + [spec(side, 1) for side in sides],
        out_specs=[
            pl.BlockSpec((row_parts, col_parts, step, count, cols), lambda s: (0, 0, s, 0, 0))
            for _, count in wanted
        ],
        out_shape=[
            jax.ShapeDtypeStruct((row_parts, col_parts, share, count, cols), jnp.bfloat16)
            for _, count in wanted
        ],
        compiler_params=params(),
        cost_estimate=cost(share * size * size, size, 6),
    )(*lefts, *sides)
    return [out.reshape(targets, share, -1, cols) for out in outs]


def exchange(array):
    return lax.all_to_all(array, ("row", "chan"), split_axis=0, concat_axis=0, tiled=True)


def local(mesh, pair, pair_mask, chain_ids, chain_embed, proj_weights, gate_weights, out_weights):
    rows, cols, width = pair.shape
    row_parts, col_parts = mesh.shape["row"], mesh.shape["chan"]
    targets = row_parts * col_parts
    hidden = out_weights.shape[1]
    block = 16
    row_chain, col_chain = chain_ids, chain_ids[None, :]
    embed = chain_embed
    proj, gate, back = (
        jnp.swapaxes(weight, 1, 2) for weight in (proj_weights, gate_weights, out_weights)
    )

    def pieces(sixteenths):
        blocks, spans, start = rows // block, [], 0
        for part in sixteenths:
            count = blocks * part // 16
            spans.append((start, count))
            start += count
        return spans

    def rows_of(spans):
        return [(first * block, count * block) for first, count in spans]

    sides = [
        exchange(
            start_call(
                row_chain, pair, pair_mask, col_chain, embed, proj[0], targets, block, first, count
            )
        )
        for first, count in pieces(FIRST)
    ]
    mixed = []
    for span in rows_of(pieces(MIDDLE)):
        mixed += [exchange(part) for part in product_call(sides, 0, row_parts, col_parts, [span])]
    state, sides = None, []
    for (first, count), part in zip(pieces(MIDDLE), mixed, strict=True):
        state, part = middle_call(
            row_chain, part.reshape(hidden, -1, cols), pair, pair_mask, col_chain, embed,
            gate[0], back[0], proj[1], targets, block, first, count, state,
        )
        sides.append(exchange(part))
    mixed = [
        exchange(part)
        for part in product_call(sides, 1, row_parts, col_parts, rows_of(pieces(LAST)))
    ]
    updated = None
    for (first, count), part in zip(pieces(LAST), mixed, strict=True):
        updated = end_call(
            part.reshape(hidden, -1, cols), state, gate[1], back[1], block, first, count, rows, updated
        )
    return updated


def solution(mesh):
    placed = (
        P(("grp", "row"), "chan", None),
        P(("grp", "row"), "chan"),
        P("grp"),
        P(),
        P(),
        P(),
        P(),
    )
    return jax.shard_map(
        functools.partial(local, mesh),
        mesh=mesh,
        in_specs=placed,
        out_specs=P(("grp", "row"), "chan", None),
        check_vma=False,
    )
```

```python
import functools
import math

import jax
import jax.numpy as jnp
from jax import lax
from jax.experimental import pallas as pl
from jax.experimental.pallas import tpu as pltpu
from jax.sharding import PartitionSpec as P

EPS = 1e-05
LANES = 128
CHANNELS = 4
VMEM = 60 * 1024 * 1024
FIRST, MIDDLE, LAST = (4, 12), (4, 12), (12, 4)


def sigmoid(x):
    return 0.5 * jnp.tanh(0.5 * x) + 0.5


def norm_channels(values):
    scale = 1.0 / values.shape[0]
    mean = jnp.sum(values, axis=0, keepdims=True) * scale
    centred = values - mean
    variance = jnp.sum(centred * centred, axis=0, keepdims=True) * scale
    return centred * lax.rsqrt(variance + EPS)


def dot(a, b):
    return jnp.dot(a, b, preferred_element_type=jnp.float32)


def same_chain(chains, chain_row, cols, rows, i):
    start = pl.multiple_of(lax.axis_index("chan") * cols, cols)
    return chain_row[:, pl.ds(start, cols)] == chains[lax.axis_index("row") * rows + i]


def turn_embed(embed_ref, embed_scr):
    _, width, cols = embed_scr.shape
    for kind in range(2):
        rows = jnp.broadcast_to(embed_ref[kind : kind + 1, :], (cols, width))
        embed_scr[kind] = rows.T


def first_state(pair_ref, same_row, embed_scr, i):
    turned = pair_ref[i].astype(jnp.float32).T
    return turned + jnp.where(same_row, embed_scr[1], embed_scr[0])


def put_row(scratch, i, rows, values):
    for part in range(values.shape[1] // LANES):
        scratch[part, pl.ds(i, values.shape[0], stride=rows), :] = values[
            :, part * LANES : (part + 1) * LANES
        ]


def get_row(scratch, i, rows, channels):
    return jnp.concatenate(
        [scratch[part, pl.ds(i, channels, stride=rows), :] for part in range(scratch.shape[0])],
        axis=1,
    )


def project_row(normed, mask_row, weight_ref, left_scr, right_scr, i, rows):
    hidden = weight_ref.shape[0] // 4
    proj = dot(weight_ref[...], normed)
    put_row(left_scr, i, rows, sigmoid(proj[:hidden]) * proj[hidden : 2 * hidden] * mask_row)
    put_row(
        right_scr, i, rows, sigmoid(proj[2 * hidden : 3 * hidden]) * proj[3 * hidden :] * mask_row
    )


def write_sides(left_scr, right_scr, out_ref):
    targets, _, share, rows, cols = out_ref.shape
    for side, scratch in enumerate((left_scr, right_scr)):
        for part in range(cols // LANES):
            out_ref[:, side, :, :, part * LANES : (part + 1) * LANES] = (
                scratch[part, : targets * share * rows, :]
                .astype(jnp.bfloat16)
                .reshape(targets, share, rows, LANES)
            )


def read_mixed(mixed_ref, scratch):
    used = mixed_ref.shape[0] * mixed_ref.shape[1]
    for part in range(scratch.shape[0]):
        scratch[part, :used, :] = (
            mixed_ref[:, :, part * LANES : (part + 1) * LANES]
            .astype(jnp.float32)
            .reshape(used, LANES)
        )


def start_kernel(
    first, total_rows, row_chain, pair_ref, mask_ref, col_chain, embed_ref, proj_ref, out_ref, left_scr, right_scr, embed_scr
):
    rows = pair_ref.shape[0]
    step = pl.program_id(0) + first
    turn_embed(embed_ref, embed_scr)

    @pl.loop(0, rows, unroll=4)
    def _(i):
        same = same_chain(row_chain, col_chain, pair_ref.shape[1], total_rows, step * rows + i)
        state = first_state(pair_ref, same, embed_scr, i)
        normed = norm_channels(state).astype(jnp.bfloat16)
        mask_row = mask_ref[pl.ds(i, 1), :].astype(jnp.float32)
        project_row(normed, mask_row, proj_ref, left_scr, right_scr, i, rows)

    write_sides(left_scr, right_scr, out_ref)


def middle_kernel(
    first, total_rows, row_chain, mixed_ref, pair_ref, mask_ref, col_chain, embed_ref, gate_ref, back_ref, proj_ref,
    state_ref, out_ref, mixed_scr, left_scr, right_scr, embed_scr,
):
    rows = pair_ref.shape[0]
    channels = mixed_ref.shape[0]
    step = pl.program_id(0) + first
    turn_embed(embed_ref, embed_scr)
    read_mixed(mixed_ref, mixed_scr)

    @pl.loop(0, rows, unroll=4)
    def _(i):
        same = same_chain(row_chain, col_chain, pair_ref.shape[1], total_rows, step * rows + i)
        state = first_state(pair_ref, same, embed_scr, i)
        normed = norm_channels(state).astype(jnp.bfloat16)
        gate = sigmoid(dot(gate_ref[...], normed))
        mixnorm = norm_channels(get_row(mixed_scr, i, rows, channels)).astype(jnp.bfloat16)
        state = state + gate * dot(back_ref[...], mixnorm)
        state_ref[i] = state
        normed = norm_channels(state).astype(jnp.bfloat16)
        mask_row = mask_ref[pl.ds(i, 1), :].astype(jnp.float32)
        project_row(normed, mask_row, proj_ref, left_scr, right_scr, i, rows)

    write_sides(left_scr, right_scr, out_ref)


def end_kernel(mixed_ref, state_ref, gate_ref, back_ref, out_ref, mixed_scr):
    rows = state_ref.shape[0]
    channels = mixed_ref.shape[0]
    read_mixed(mixed_ref, mixed_scr)

    @pl.loop(0, rows, unroll=4)
    def _(i):
        state = state_ref[i]
        normed = norm_channels(state).astype(jnp.bfloat16)
        gate = sigmoid(dot(gate_ref[...], normed))
        mixnorm = norm_channels(get_row(mixed_scr, i, rows, channels)).astype(jnp.bfloat16)
        state = state + gate * dot(back_ref[...], mixnorm)
        out_ref[i] = state.T.astype(jnp.bfloat16)


def middle_kernel_onto(first, total_rows, *refs):
    middle_kernel(first, total_rows, *refs[:9], *refs[10:])


def end_kernel_onto(mixed_ref, state_ref, gate_ref, back_ref, earlier_ref, out_ref, mixed_scr):
    del earlier_ref
    end_kernel(mixed_ref, state_ref, gate_ref, back_ref, out_ref, mixed_scr)


def cost(pairs, multiplies, bytes_each):
    return pl.CostEstimate(
        flops=2 * pairs * multiplies, bytes_accessed=pairs * bytes_each, transcendentals=0
    )


def whole(array):
    return pl.BlockSpec(array.shape, lambda *_: (0,) * array.ndim)


def params():
    return pltpu.CompilerParams(vmem_limit_bytes=VMEM)


def scratches(count, channels, rows, cols):
    return [pltpu.VMEM((cols // LANES, (channels + 1) * rows, LANES), jnp.float32)] * count


SMEM_SPEC = pl.BlockSpec(memory_space=pltpu.SMEM)


def start_call(row_chain, pair, mask, col_chain, embed, proj, targets, block, first, count):
    _, cols, width = pair.shape
    hidden = proj.shape[0] // 4
    share = hidden // targets
    return pl.pallas_call(
        functools.partial(start_kernel, first, pair.shape[0]),
        grid=(count,),
        in_specs=[
            SMEM_SPEC,
            pl.BlockSpec((block, cols, width), lambda s: (s + first, 0, 0)),
            pl.BlockSpec((block, cols), lambda s: (s + first, 0)),
            whole(col_chain),
            whole(embed),
            whole(proj),
        ],
        out_specs=pl.BlockSpec((targets, 2, share, block, cols), lambda s: (0, 0, 0, s, 0)),
        out_shape=jax.ShapeDtypeStruct((targets, 2, share, count * block, cols), jnp.bfloat16),
        scratch_shapes=scratches(2, hidden, block, cols) + [pltpu.VMEM((2, width, cols), jnp.float32)],
        compiler_params=params(),
        cost_estimate=cost(count * block * cols, 5 * width * width, 4 * width),
    )(row_chain, pair, mask, col_chain, embed, proj)


def middle_call(
    row_chain, mixed, pair, mask, col_chain, embed, gate, back, proj, targets, block, first, count, earlier
):
    rows, cols, width = pair.shape
    hidden = proj.shape[0] // 4
    share = hidden // targets
    operands = [row_chain, mixed, pair, mask, col_chain, embed, gate, back, proj]
    in_specs = [
        SMEM_SPEC,
        pl.BlockSpec((hidden, block, cols), lambda s: (0, s, 0)),
        pl.BlockSpec((block, cols, width), lambda s: (s + first, 0, 0)),
        pl.BlockSpec((block, cols), lambda s: (s + first, 0)),
        whole(col_chain),
        whole(embed),
        whole(gate),
        whole(back),
        whole(proj),
    ]
    kernel, aliases = middle_kernel, {}
    if earlier is not None:
        kernel, aliases = middle_kernel_onto, {9: 0}
        operands.append(earlier)
        in_specs.append(pl.BlockSpec(memory_space=pl.ANY))
    return pl.pallas_call(
        functools.partial(kernel, first, rows),
        grid=(count,),
        in_specs=in_specs,
        out_specs=[
            pl.BlockSpec((block, width, cols), lambda s: (s + first, 0, 0)),
            pl.BlockSpec((targets, 2, share, block, cols), lambda s: (0, 0, 0, s, 0)),
        ],
        out_shape=[
            jax.ShapeDtypeStruct((rows, width, cols), jnp.float32),
            jax.ShapeDtypeStruct((targets, 2, share, count * block, cols), jnp.bfloat16),
        ],
        scratch_shapes=scratches(3, hidden, block, cols) + [pltpu.VMEM((2, width, cols), jnp.float32)],
        input_output_aliases=aliases,
        compiler_params=params(),
        cost_estimate=cost(count * block * cols, 8 * width * width, 12 * width),
    )(*operands)


def end_call(mixed, state, gate, back, block, first, count, rows, earlier):
    _, width, cols = state.shape
    hidden = mixed.shape[0]
    kernel = end_kernel
    operands = [mixed, state, gate, back]
    in_specs = [
        pl.BlockSpec((hidden, block, cols), lambda s: (0, s, 0)),
        pl.BlockSpec((block, width, cols), lambda s: (s + first, 0, 0)),
        whole(gate),
        whole(back),
    ]
    aliases = {}
    if earlier is not None:
        kernel = end_kernel_onto
        operands.append(earlier)
        in_specs.append(pl.BlockSpec(memory_space=pl.ANY))
        aliases = {4: 0}
    return pl.pallas_call(
        kernel,
        grid=(count,),
        in_specs=in_specs,
        out_specs=pl.BlockSpec((block, cols, width), lambda s: (s + first, 0, 0)),
        out_shape=jax.ShapeDtypeStruct((rows, cols, width), jnp.bfloat16),
        scratch_shapes=scratches(1, hidden, block, cols),
        input_output_aliases=aliases,
        compiler_params=params(),
        cost_estimate=cost(count * block * cols, 2 * width * width, 8 * width),
    )(*operands)


def product_kernel(update, lefts, rights, wanted, *refs):
    for channel in range(refs[0].shape[3]):
        product_channel(channel, update, lefts, rights, wanted, *refs)


def product_channel(channel, update, lefts, rights, wanted, *refs):
    left_refs, right_refs, outs = refs[:lefts], refs[lefts : lefts + rights], refs[lefts + rights :]
    row_parts, col_parts = right_refs[0].shape[:2]
    cols = right_refs[0].shape[-1]

    def side(held, part):
        held = [ref[:, part, 0, channel] for ref in held]
        return held[0] if len(held) == 1 else jnp.concatenate(held, axis=1)

    if update == 0:
        right = [side(right_refs, part).reshape(-1, cols) for part in range(col_parts)]
        for (first, count), out in zip(wanted, outs, strict=True):
            total = None
            for part in range(col_parts):
                left = side(left_refs, part)[:, first : first + count].reshape(-1, cols)
                term = lax.dot_general(
                    left, right[part], (((1,), (1,)), ((), ())), preferred_element_type=jnp.float32
                )
                total = term if total is None else total + term
            mixed = total.astype(jnp.bfloat16).reshape(row_parts, count, -1)
            for part in range(col_parts):
                out[:, part, channel] = mixed[:, :, part * cols : (part + 1) * cols]
    else:
        left = jnp.concatenate(
            [side(left_refs, part).reshape(-1, cols) for part in range(col_parts)], axis=1
        )
        for part in range(col_parts):
            mixed = lax.dot_general(
                left, side(right_refs, part).reshape(-1, cols), (((0,), (0,)), ((), ())),
                preferred_element_type=jnp.float32,
            ).astype(jnp.bfloat16)
            mixed = mixed.reshape(row_parts, -1, cols)
            for (first, count), out in zip(wanted, outs, strict=True):
                out[:, part, channel] = mixed[:, first : first + count]


def product_call(sides, update, row_parts, col_parts, wanted):
    targets, _, share, _, cols = sides[0].shape
    sides = [side.reshape(row_parts, col_parts, 2, share, -1, cols) for side in sides]
    size = row_parts * sum(side.shape[4] for side in sides)
    lefts, shift = sides, 0
    if update == 0:
        lefts, start = [], 0
        first, last = wanted[0][0], wanted[-1][0] + wanted[-1][1]
        for side in sides:
            end = start + side.shape[4]
            if end <= first:
                shift = end
            elif start < last:
                lefts.append(side)
            start = end
    wanted = [(first - shift, count) for first, count in wanted]
    step = math.gcd(share, CHANNELS)

    def spec(side, which):
        return pl.BlockSpec(
            (row_parts, col_parts, 1, step, side.shape[4], cols), lambda s: (0, 0, which, s, 0, 0)
        )

    outs = pl.pallas_call(
        functools.partial(product_kernel, update, len(lefts), len(sides), wanted),
        grid=(share // step,),
        in_specs=[spec(side, 0) for side in lefts] + [spec(side, 1) for side in sides],
        out_specs=[
            pl.BlockSpec((row_parts, col_parts, step, count, cols), lambda s: (0, 0, s, 0, 0))
            for _, count in wanted
        ],
        out_shape=[
            jax.ShapeDtypeStruct((row_parts, col_parts, share, count, cols), jnp.bfloat16)
            for _, count in wanted
        ],
        compiler_params=params(),
        cost_estimate=cost(share * size * size, size, 6),
    )(*lefts, *sides)
    return [out.reshape(targets, share, -1, cols) for out in outs]


def exchange(array):
    return lax.all_to_all(array, ("row", "chan"), split_axis=0, concat_axis=0, tiled=True)


def local(mesh, pair, pair_mask, chain_ids, chain_embed, proj_weights, gate_weights, out_weights):
    rows, cols, width = pair.shape
    row_parts, col_parts = mesh.shape["row"], mesh.shape["chan"]
    targets = row_parts * col_parts
    hidden = out_weights.shape[1]
    block = 16
    row_chain, col_chain = chain_ids, chain_ids[None, :]
    embed = chain_embed
    proj, gate, back = (
        jnp.swapaxes(weight, 1, 2) for weight in (proj_weights, gate_weights, out_weights)
    )

    def pieces(sixteenths):
        blocks, spans, start = rows // block, [], 0
        for part in sixteenths:
            count = blocks * part // 16
            spans.append((start, count))
            start += count
        return spans

    def rows_of(spans):
        return [(first * block, count * block) for first, count in spans]

    sides = [
        exchange(
            start_call(
                row_chain, pair, pair_mask, col_chain, embed, proj[0], targets, block, first, count
            )
        )
        for first, count in pieces(FIRST)
    ]
    mixed = []
    for span in rows_of(pieces(MIDDLE)):
        mixed += [exchange(part) for part in product_call(sides, 0, row_parts, col_parts, [span])]
    state, sides = None, []
    for (first, count), part in zip(pieces(MIDDLE), mixed, strict=True):
        state, part = middle_call(
            row_chain, part.reshape(hidden, -1, cols), pair, pair_mask, col_chain, embed,
            gate[0], back[0], proj[1], targets, block, first, count, state,
        )
        sides.append(exchange(part))
    mixed = [
        exchange(part)
        for part in product_call(sides, 1, row_parts, col_parts, rows_of(pieces(LAST)))
    ]
    updated = None
    for (first, count), part in zip(pieces(LAST), mixed, strict=True):
        updated = end_call(
            part.reshape(hidden, -1, cols), state, gate[1], back[1], block, first, count, rows, updated
        )
    return updated


def solution(mesh):
    placed = (
        P(("grp", "row"), "chan", None),
        P(("grp", "row"), "chan"),
        P("grp"),
        P(),
        P(),
        P(),
        P(),
    )
    return jax.shard_map(
        functools.partial(local, mesh),
        mesh=mesh,
        in_specs=placed,
        out_specs=P(("grp", "row"), "chan", None),
        check_vma=False,
    )
```

```python
import functools
import math

import jax
import jax.numpy as jnp
from jax import lax
from jax.experimental import pallas as pl
from jax.experimental.pallas import tpu as pltpu
from jax.sharding import PartitionSpec as P

EPS = 1e-05
LANES = 128
CHANNELS = 4
VMEM = 60 * 1024 * 1024
FIRST, MIDDLE, LAST = (4, 12), (4, 12), (12, 4)


def sigmoid(x):
    return 0.5 * jnp.tanh(0.5 * x) + 0.5


def norm_channels(values):
    scale = 1.0 / values.shape[0]
    mean = jnp.sum(values, axis=0, keepdims=True) * scale
    centred = values - mean
    variance = jnp.sum(centred * centred, axis=0, keepdims=True) * scale
    return centred * lax.rsqrt(variance + EPS)


def dot(a, b):
    return jnp.dot(a, b, preferred_element_type=jnp.float32)


def same_chain(chains, chain_row, cols, rows, i):
    start = pl.multiple_of(lax.axis_index("chan") * cols, cols)
    return chain_row[:, pl.ds(start, cols)] == chains[lax.axis_index("row") * rows + i]


def turn_embed(embed_ref, embed_scr):
    _, width, cols = embed_scr.shape
    for kind in range(2):
        rows = jnp.broadcast_to(embed_ref[kind : kind + 1, :], (cols, width))
        embed_scr[kind] = rows.T


def first_state(pair_ref, same_row, embed_scr, i):
    turned = pair_ref[i].astype(jnp.float32).T
    return turned + jnp.where(same_row, embed_scr[1], embed_scr[0])


def put_row(scratch, i, rows, values):
    for part in range(values.shape[1] // LANES):
        scratch[part, pl.ds(i, values.shape[0], stride=rows), :] = values[
            :, part * LANES : (part + 1) * LANES
        ]


def get_row(scratch, i, rows, channels):
    return jnp.concatenate(
        [scratch[part, pl.ds(i, channels, stride=rows), :] for part in range(scratch.shape[0])],
        axis=1,
    )


def project_row(normed, mask_row, weight_ref, left_scr, right_scr, i, rows):
    hidden = weight_ref.shape[0] // 4
    proj = dot(weight_ref[...], normed)
    put_row(left_scr, i, rows, sigmoid(proj[:hidden]) * proj[hidden : 2 * hidden] * mask_row)
    put_row(
        right_scr, i, rows, sigmoid(proj[2 * hidden : 3 * hidden]) * proj[3 * hidden :] * mask_row
    )


def write_sides(left_scr, right_scr, out_ref):
    targets, _, share, rows, cols = out_ref.shape
    for side, scratch in enumerate((left_scr, right_scr)):
        for part in range(cols // LANES):
            out_ref[:, side, :, :, part * LANES : (part + 1) * LANES] = (
                scratch[part, : targets * share * rows, :]
                .astype(jnp.bfloat16)
                .reshape(targets, share, rows, LANES)
            )


def read_mixed(mixed_ref, scratch):
    used = mixed_ref.shape[0] * mixed_ref.shape[1]
    for part in range(scratch.shape[0]):
        scratch[part, :used, :] = (
            mixed_ref[:, :, part * LANES : (part + 1) * LANES]
            .astype(jnp.float32)
            .reshape(used, LANES)
        )


def start_kernel(
    first, total_rows, row_chain, pair_ref, mask_ref, col_chain, embed_ref, proj_ref, out_ref, left_scr, right_scr, embed_scr
):
    rows = pair_ref.shape[0]
    step = pl.program_id(0) + first
    turn_embed(embed_ref, embed_scr)

    @pl.loop(0, rows, unroll=8)
    def _(i):
        same = same_chain(row_chain, col_chain, pair_ref.shape[1], total_rows, step * rows + i)
        state = first_state(pair_ref, same, embed_scr, i)
        normed = norm_channels(state).astype(jnp.bfloat16)
        mask_row = mask_ref[pl.ds(i, 1), :].astype(jnp.float32)
        project_row(normed, mask_row, proj_ref, left_scr, right_scr, i, rows)

    write_sides(left_scr, right_scr, out_ref)


def middle_kernel(
    first, total_rows, row_chain, mixed_ref, pair_ref, mask_ref, col_chain, embed_ref, gate_ref, back_ref, proj_ref,
    state_ref, out_ref, mixed_scr, left_scr, right_scr, embed_scr,
):
    rows = pair_ref.shape[0]
    channels = mixed_ref.shape[0]
    step = pl.program_id(0) + first
    turn_embed(embed_ref, embed_scr)
    read_mixed(mixed_ref, mixed_scr)

    @pl.loop(0, rows, unroll=8)
    def _(i):
        same = same_chain(row_chain, col_chain, pair_ref.shape[1], total_rows, step * rows + i)
        state = first_state(pair_ref, same, embed_scr, i)
        normed = norm_channels(state).astype(jnp.bfloat16)
        gate = sigmoid(dot(gate_ref[...], normed))
        mixnorm = norm_channels(get_row(mixed_scr, i, rows, channels)).astype(jnp.bfloat16)
        state = state + gate * dot(back_ref[...], mixnorm)
        state_ref[i] = state
        normed = norm_channels(state).astype(jnp.bfloat16)
        mask_row = mask_ref[pl.ds(i, 1), :].astype(jnp.float32)
        project_row(normed, mask_row, proj_ref, left_scr, right_scr, i, rows)

    write_sides(left_scr, right_scr, out_ref)


def end_kernel(mixed_ref, state_ref, gate_ref, back_ref, out_ref, mixed_scr):
    rows = state_ref.shape[0]
    channels = mixed_ref.shape[0]
    read_mixed(mixed_ref, mixed_scr)

    @pl.loop(0, rows, unroll=8)
    def _(i):
        state = state_ref[i]
        normed = norm_channels(state).astype(jnp.bfloat16)
        gate = sigmoid(dot(gate_ref[...], normed))
        mixnorm = norm_channels(get_row(mixed_scr, i, rows, channels)).astype(jnp.bfloat16)
        state = state + gate * dot(back_ref[...], mixnorm)
        out_ref[i] = state.T.astype(jnp.bfloat16)


def middle_kernel_onto(first, total_rows, *refs):
    middle_kernel(first, total_rows, *refs[:9], *refs[10:])


def end_kernel_onto(mixed_ref, state_ref, gate_ref, back_ref, earlier_ref, out_ref, mixed_scr):
    del earlier_ref
    end_kernel(mixed_ref, state_ref, gate_ref, back_ref, out_ref, mixed_scr)


def cost(pairs, multiplies, bytes_each):
    return pl.CostEstimate(
        flops=2 * pairs * multiplies, bytes_accessed=pairs * bytes_each, transcendentals=0
    )


def whole(array):
    return pl.BlockSpec(array.shape, lambda *_: (0,) * array.ndim)


def params():
    return pltpu.CompilerParams(vmem_limit_bytes=VMEM)


def scratches(count, channels, rows, cols):
    return [pltpu.VMEM((cols // LANES, (channels + 1) * rows, LANES), jnp.float32)] * count


SMEM_SPEC = pl.BlockSpec(memory_space=pltpu.SMEM)


def start_call(row_chain, pair, mask, col_chain, embed, proj, targets, block, first, count):
    _, cols, width = pair.shape
    hidden = proj.shape[0] // 4
    share = hidden // targets
    return pl.pallas_call(
        functools.partial(start_kernel, first, pair.shape[0]),
        grid=(count,),
        in_specs=[
            SMEM_SPEC,
            pl.BlockSpec((block, cols, width), lambda s: (s + first, 0, 0)),
            pl.BlockSpec((block, cols), lambda s: (s + first, 0)),
            whole(col_chain),
            whole(embed),
            whole(proj),
        ],
        out_specs=pl.BlockSpec((targets, 2, share, block, cols), lambda s: (0, 0, 0, s, 0)),
        out_shape=jax.ShapeDtypeStruct((targets, 2, share, count * block, cols), jnp.bfloat16),
        scratch_shapes=scratches(2, hidden, block, cols) + [pltpu.VMEM((2, width, cols), jnp.float32)],
        compiler_params=params(),
        cost_estimate=cost(count * block * cols, 5 * width * width, 4 * width),
    )(row_chain, pair, mask, col_chain, embed, proj)


def middle_call(
    row_chain, mixed, pair, mask, col_chain, embed, gate, back, proj, targets, block, first, count, earlier
):
    rows, cols, width = pair.shape
    hidden = proj.shape[0] // 4
    share = hidden // targets
    operands = [row_chain, mixed, pair, mask, col_chain, embed, gate, back, proj]
    in_specs = [
        SMEM_SPEC,
        pl.BlockSpec((hidden, block, cols), lambda s: (0, s, 0)),
        pl.BlockSpec((block, cols, width), lambda s: (s + first, 0, 0)),
        pl.BlockSpec((block, cols), lambda s: (s + first, 0)),
        whole(col_chain),
        whole(embed),
        whole(gate),
        whole(back),
        whole(proj),
    ]
    kernel, aliases = middle_kernel, {}
    if earlier is not None:
        kernel, aliases = middle_kernel_onto, {9: 0}
        operands.append(earlier)
        in_specs.append(pl.BlockSpec(memory_space=pl.ANY))
    return pl.pallas_call(
        functools.partial(kernel, first, rows),
        grid=(count,),
        in_specs=in_specs,
        out_specs=[
            pl.BlockSpec((block, width, cols), lambda s: (s + first, 0, 0)),
            pl.BlockSpec((targets, 2, share, block, cols), lambda s: (0, 0, 0, s, 0)),
        ],
        out_shape=[
            jax.ShapeDtypeStruct((rows, width, cols), jnp.float32),
            jax.ShapeDtypeStruct((targets, 2, share, count * block, cols), jnp.bfloat16),
        ],
        scratch_shapes=scratches(3, hidden, block, cols) + [pltpu.VMEM((2, width, cols), jnp.float32)],
        input_output_aliases=aliases,
        compiler_params=params(),
        cost_estimate=cost(count * block * cols, 8 * width * width, 12 * width),
    )(*operands)


def end_call(mixed, state, gate, back, block, first, count, rows, earlier):
    _, width, cols = state.shape
    hidden = mixed.shape[0]
    kernel = end_kernel
    operands = [mixed, state, gate, back]
    in_specs = [
        pl.BlockSpec((hidden, block, cols), lambda s: (0, s, 0)),
        pl.BlockSpec((block, width, cols), lambda s: (s + first, 0, 0)),
        whole(gate),
        whole(back),
    ]
    aliases = {}
    if earlier is not None:
        kernel = end_kernel_onto
        operands.append(earlier)
        in_specs.append(pl.BlockSpec(memory_space=pl.ANY))
        aliases = {4: 0}
    return pl.pallas_call(
        kernel,
        grid=(count,),
        in_specs=in_specs,
        out_specs=pl.BlockSpec((block, cols, width), lambda s: (s + first, 0, 0)),
        out_shape=jax.ShapeDtypeStruct((rows, cols, width), jnp.bfloat16),
        scratch_shapes=scratches(1, hidden, block, cols),
        input_output_aliases=aliases,
        compiler_params=params(),
        cost_estimate=cost(count * block * cols, 2 * width * width, 8 * width),
    )(*operands)


def product_kernel(update, lefts, rights, wanted, *refs):
    for channel in range(refs[0].shape[3]):
        product_channel(channel, update, lefts, rights, wanted, *refs)


def product_channel(channel, update, lefts, rights, wanted, *refs):
    left_refs, right_refs, outs = refs[:lefts], refs[lefts : lefts + rights], refs[lefts + rights :]
    row_parts, col_parts = right_refs[0].shape[:2]
    cols = right_refs[0].shape[-1]

    def side(held, part):
        held = [ref[:, part, 0, channel] for ref in held]
        return held[0] if len(held) == 1 else jnp.concatenate(held, axis=1)

    if update == 0:
        right = [side(right_refs, part).reshape(-1, cols) for part in range(col_parts)]
        for (first, count), out in zip(wanted, outs, strict=True):
            total = None
            for part in range(col_parts):
                left = side(left_refs, part)[:, first : first + count].reshape(-1, cols)
                term = lax.dot_general(
                    left, right[part], (((1,), (1,)), ((), ())), preferred_element_type=jnp.float32
                )
                total = term if total is None else total + term
            mixed = total.astype(jnp.bfloat16).reshape(row_parts, count, -1)
            for part in range(col_parts):
                out[:, part, channel] = mixed[:, :, part * cols : (part + 1) * cols]
    else:
        left = jnp.concatenate(
            [side(left_refs, part).reshape(-1, cols) for part in range(col_parts)], axis=1
        )
        for part in range(col_parts):
            mixed = lax.dot_general(
                left, side(right_refs, part).reshape(-1, cols), (((0,), (0,)), ((), ())),
                preferred_element_type=jnp.float32,
            ).astype(jnp.bfloat16)
            mixed = mixed.reshape(row_parts, -1, cols)
            for (first, count), out in zip(wanted, outs, strict=True):
                out[:, part, channel] = mixed[:, first : first + count]


def product_call(sides, update, row_parts, col_parts, wanted):
    targets, _, share, _, cols = sides[0].shape
    sides = [side.reshape(row_parts, col_parts, 2, share, -1, cols) for side in sides]
    size = row_parts * sum(side.shape[4] for side in sides)
    lefts, shift = sides, 0
    if update == 0:
        lefts, start = [], 0
        first, last = wanted[0][0], wanted[-1][0] + wanted[-1][1]
        for side in sides:
            end = start + side.shape[4]
            if end <= first:
                shift = end
            elif start < last:
                lefts.append(side)
            start = end
    wanted = [(first - shift, count) for first, count in wanted]
    step = math.gcd(share, CHANNELS)

    def spec(side, which):
        return pl.BlockSpec(
            (row_parts, col_parts, 1, step, side.shape[4], cols), lambda s: (0, 0, which, s, 0, 0)
        )

    outs = pl.pallas_call(
        functools.partial(product_kernel, update, len(lefts), len(sides), wanted),
        grid=(share // step,),
        in_specs=[spec(side, 0) for side in lefts] + [spec(side, 1) for side in sides],
        out_specs=[
            pl.BlockSpec((row_parts, col_parts, step, count, cols), lambda s: (0, 0, s, 0, 0))
            for _, count in wanted
        ],
        out_shape=[
            jax.ShapeDtypeStruct((row_parts, col_parts, share, count, cols), jnp.bfloat16)
            for _, count in wanted
        ],
        compiler_params=params(),
        cost_estimate=cost(share * size * size, size, 6),
    )(*lefts, *sides)
    return [out.reshape(targets, share, -1, cols) for out in outs]


def exchange(array):
    return lax.all_to_all(array, ("row", "chan"), split_axis=0, concat_axis=0, tiled=True)


def local(mesh, pair, pair_mask, chain_ids, chain_embed, proj_weights, gate_weights, out_weights):
    rows, cols, width = pair.shape
    row_parts, col_parts = mesh.shape["row"], mesh.shape["chan"]
    targets = row_parts * col_parts
    hidden = out_weights.shape[1]
    block = 16
    row_chain, col_chain = chain_ids, chain_ids[None, :]
    embed = chain_embed
    proj, gate, back = (
        jnp.swapaxes(weight, 1, 2) for weight in (proj_weights, gate_weights, out_weights)
    )

    def pieces(sixteenths):
        blocks, spans, start = rows // block, [], 0
        for part in sixteenths:
            count = blocks * part // 16
            spans.append((start, count))
            start += count
        return spans

    def rows_of(spans):
        return [(first * block, count * block) for first, count in spans]

    sides = [
        exchange(
            start_call(
                row_chain, pair, pair_mask, col_chain, embed, proj[0], targets, block, first, count
            )
        )
        for first, count in pieces(FIRST)
    ]
    mixed = []
    for span in rows_of(pieces(MIDDLE)):
        mixed += [exchange(part) for part in product_call(sides, 0, row_parts, col_parts, [span])]
    state, sides = None, []
    for (first, count), part in zip(pieces(MIDDLE), mixed, strict=True):
        state, part = middle_call(
            row_chain, part.reshape(hidden, -1, cols), pair, pair_mask, col_chain, embed,
            gate[0], back[0], proj[1], targets, block, first, count, state,
        )
        sides.append(exchange(part))
    mixed = [
        exchange(part)
        for part in product_call(sides, 1, row_parts, col_parts, rows_of(pieces(LAST)))
    ]
    updated = None
    for (first, count), part in zip(pieces(LAST), mixed, strict=True):
        updated = end_call(
            part.reshape(hidden, -1, cols), state, gate[1], back[1], block, first, count, rows, updated
        )
    return updated


def solution(mesh):
    placed = (
        P(("grp", "row"), "chan", None),
        P(("grp", "row"), "chan"),
        P("grp"),
        P(),
        P(),
        P(),
        P(),
    )
    return jax.shard_map(
        functools.partial(local, mesh),
        mesh=mesh,
        in_specs=placed,
        out_specs=P(("grp", "row"), "chan", None),
        check_vma=False,
    )
```
